32 devices in a mesh: replica: 2 (over y), fsdp: 4 (over x, core), seq: 4 (over z).
Axes of the slice: x: 2, y: 2, z: 4, core: 2. Of those that a mesh axis runs over, the one named last changes fastest.
Arguments:
- tokens: bfloat16 [8, 1024, 768], P(('replica', 'fsdp'), 'seq'), may hold values from -6 to 6
- cotangent: bfloat16 [8, 1024, 768], P(('replica', 'fsdp'), 'seq'), may hold values from -6 to 6
- expert_ids: int32 [8, 1024, 1], P(('replica', 'fsdp'), 'seq'), may hold values from 0 to 3; in each aligned block of 256 rows (0 to 255, 256 to 511, ..., all dimensions but the last counted through in order) at most 80 rows name the same one
- attn_gain: bfloat16 [768], P(('fsdp', 'seq')), may hold values from 0.5 to 1.5
- qkv_weight: bfloat16 [768, 2304], P(('fsdp', 'seq')), may hold values from -0.21875 to 0.21875
- output_weight: bfloat16 [768, 768], P(('fsdp', 'seq')), may hold values from -4 to 4
- bias_table: bfloat16 [384], P(('fsdp', 'seq')), may hold values from -4 to 4
- ffn_gain: bfloat16 [768], P(('fsdp', 'seq')), may hold values from 0.5 to 1.5
- router_projection_weight: bfloat16 [768, 4], P(('fsdp', 'seq')), may hold values from -0.15625 to 0.15625
- expert_in: bfloat16 [3072, 4, 768], P(('fsdp', 'seq')), may hold values from -0.21875 to 0.21875
- expert_out: bfloat16 [3072, 4, 768], P(('fsdp', 'seq')), may hold values from -0.4375 to 0.4375
Outputs:
- layer_out: bfloat16 [8, 1024, 768], P(('replica', 'fsdp'), 'seq')
- grad_tokens: bfloat16 [8, 1024, 768], P(('replica', 'fsdp'), 'seq')
- grad_attn_gain: float32 [768], P(('fsdp', 'seq'))
- grad_qkv_weight: float32 [768, 2304], P(('fsdp', 'seq'))
- grad_output_weight: float32 [768, 768], P(('fsdp', 'seq'))
- grad_bias_table: float32 [384], P(('fsdp', 'seq'))
- grad_ffn_gain: float32 [768], P(('fsdp', 'seq'))
- grad_router_weight: float32 [768, 4], P(('fsdp', 'seq'))
- grad_expert_in: float32 [3072, 4, 768], P(('fsdp', 'seq'))
- grad_expert_out: float32 [3072, 4, 768], P(('fsdp', 'seq'))
The draws below stay inside these ranges and needn't reach their ends.
Inputs may be any that keep to these rules, and one draw needn't show every extreme that they name: `expert_ids`: in each aligned block of 256 positions of a sequence no expert is named by more than 80 tokens, and in every draw some block has an expert named by exactly 80.
All inputs are finite; a program needn't handle non-finite values.
Results may differ from the reference program's by a relative error of at most 0.017.
Values may be sent and summed in bfloat16 or wider, within the bound.
No kernel may reach another device: no remote copies, remote signals or barrier semaphores. Data moves between devices by JAX's collectives and lax.ppermute only.
A program may use at most 192 MiB of HBM per device.

```python
import math
import jax
import jax.numpy as jnp
import numpy as np
from jax import lax

D = 768
HEADS = 12
HEAD_DIM = 64
FF = 3072
BUCKETS = 32
EXPERTS = 4
LENGTH = 1024
TOK_SEQ = 256
CAP = 80
SEQS = 8


def level_of(rng, shape, split, low, high):
    def one(axis_at, parts):
        heights = jax.random.uniform(jax.random.fold_in(jax.random.fold_in(rng, 6), axis_at), (parts,), jnp.float32, low / len(split), high / len(split))
        return jnp.repeat(jnp.exp(heights), shape[axis_at] // parts).reshape((-1,) + (1,) * (len(shape) - axis_at - 1))

    loudness = one(*split[0])
    for cut in split[1:]:
        loudness = loudness * one(*cut)
    return loudness


def assign_block(rng, own, number, rows, count, top, bound, skew):
    ranking = jax.random.permutation(rng, count)
    heavy_load, usual = portions_of(count, rows * top, bound, skew, True), portions_of(count, rows * top, bound, skew, False)
    places = jnp.arange(count)

    def named(tallies, rotation):
        used = int((tallies > 0).sum())
        fixed = max(1, used // 4)
        shifted = fixed + (places - fixed + rotation * (used - fixed)) % max(1, count - fixed)
        return jnp.zeros((count,), jnp.int32).at[ranking[jnp.where(places < fixed, places, shifted)]].set(jnp.asarray(tallies, jnp.int32))

    tallies = jnp.where(number % 4 == 0, named(heavy_load, number // 4), named(usual, number - number // 4 - 1))
    mixed = jax.random.permutation(jax.random.fold_in(own, 3), count)
    donor, receiver = mixed[0:count // 2 * 2:2], mixed[1:count // 2 * 2:2]
    slack = jnp.minimum(tallies[donor] - 1, bound - tallies[receiver]) // 2
    slack = jnp.where((donor == ranking[0]) | (receiver == ranking[0]) | (tallies[receiver] == 0), 0, jnp.maximum(slack, 0))
    shifted = jax.random.randint(jax.random.fold_in(own, 4), (count // 2,), 0, 1 << 20) % (slack + 1)
    tallies = tallies.at[donor].add(-shifted).at[receiver].add(shifted)
    items = jnp.searchsorted(jnp.cumsum(tallies), jnp.arange(rows * top), side="right").astype(jnp.int32)
    grid = items.reshape(top, rows).T
    grid = grid[jax.random.permutation(jax.random.fold_in(own, 1), rows)]
    rotation = jax.random.randint(jax.random.fold_in(own, 2), (rows, 1), 0, top)
    return jnp.take_along_axis(grid, (jnp.arange(top)[None, :] + rotation) % top, axis=1)


def portions_of(number_of, total, bound, lean, full):
    portions = [(1 << 20) // math.isqrt(standing ** lean) + 1 for standing in range(1, number_of + 1)]
    largest = bound if full else min(bound, max(-(-total // number_of), total * portions[0] // sum(portions)))
    least = 1 if total - largest >= number_of - 1 else 0
    given, spare = [largest] + [least] * (number_of - 1), total - largest - least * (number_of - 1)
    while spare > 0:
        movable = [i for i in range(1, number_of) if given[i] < largest] or [i for i in range(1, number_of) if given[i] < bound]
        whole, left = sum([portions[i] for i in movable]), spare
        for i in movable:
            extra = min(bound - given[i], max(1, left * portions[i] // whole), spare)
            given[i] = given[i] + extra
            spare = spare - extra
    return np.array(given)


def gaussian(rng, dims, width, limit, split=(), kind=jnp.bfloat16):
    entries = jax.random.normal(rng, dims, jnp.float32) * width
    if len(split) > 0:
        entries = level_of(rng, dims, split, -0.22, 0.18) * entries
    return jnp.clip(entries, min=-limit, max=limit).astype(kind)


def setup_inputs(seed: int = 0) -> dict:
    splits = jax.random.split(jax.random.key(seed), 12)
    tokens = gaussian(splits[0], (SEQS, LENGTH, D), 1.0, 6.0, ((0, 8), (1, 4)))
    cotangent = gaussian(splits[1], (SEQS, LENGTH, D), 1.0, 6.0, ((0, 8), (1, 4)))
    expert_ids_keys = jax.random.split(jax.random.fold_in(splits[2], 1), SEQS * LENGTH // TOK_SEQ)
    expert_ids_turns = jax.random.permutation(jax.random.fold_in(splits[2], 3), SEQS * LENGTH // TOK_SEQ)
    expert_ids = jax.vmap(lambda own, number: assign_block(jax.random.fold_in(splits[2], 2), own, number, TOK_SEQ, EXPERTS, 1, CAP, 1))(expert_ids_keys, expert_ids_turns).reshape((SEQS, LENGTH, 1))
    attn_gain = jnp.clip(1.0 + 0.1 * jax.random.normal(splits[3], (D,), jnp.float32), 0.5, 1.5).astype(jnp.bfloat16)
    qkv_weight = gaussian(splits[4], (D, 3 * D), D ** -0.5, 0.21875, ((0, 16),))
    output_weight = gaussian(splits[5], (D, D), 2 ** -0.5, 4.0, ((0, 16),))
    bias_table = gaussian(splits[6], (BUCKETS * HEADS,), 1.0, 4.0, ((0, 16),))
    ffn_gain = jnp.clip(1.0 + 0.1 * jax.random.normal(splits[7], (D,), jnp.float32), 0.5, 1.5).astype(jnp.bfloat16)
    router_projection_weight = gaussian(splits[8], (D, EXPERTS), (2 * D) ** -0.5, 0.15625, ((0, 16),))
    expert_in = gaussian(splits[9], (FF, EXPERTS, D), D ** -0.5, 0.21875, ((0, 16),))
    expert_out = gaussian(splits[10], (FF, EXPERTS, D), (FF // 16) ** -0.5, 0.4375, ((0, 16),))
    return dict(tokens=tokens, cotangent=cotangent, expert_ids=expert_ids, attn_gain=attn_gain, qkv_weight=qkv_weight, output_weight=output_weight, bias_table=bias_table, ffn_gain=ffn_gain, router_projection_weight=router_projection_weight, expert_in=expert_in, expert_out=expert_out)


epsilon = 1e-06
top_expert_index = lax.Precision.HIGHEST
thresholds = (12, 16, 23, 32, 46, 64, 91)
score_scale = 0.125

@jax.custom_vjp
def low(v):
    return lax.optimization_barrier(v.astype(jnp.bfloat16)).astype(jnp.float32)

@jax.custom_vjp
def low_back(v):
    return v

def low_keep(v):
    return (low(v), None)

def low_pass(kept, grad):
    return (grad,)

def back_keep(v):
    return (v, None)

def back_low(kept, grad):
    return (low(grad),)
low.defvjp(low_keep, low_pass)
low_back.defvjp(back_keep, back_low)

def smooth_unit(values):
    return 0.5 * values * (1.0 + jnp.tanh(0.7978845608028654 * (values + 0.044715 * values * values * values)))

def bucket_of(distance):
    magnitude = jnp.abs(distance)
    far_bucket = jnp.full(distance.shape, 8, jnp.int32)
    for boundary in thresholds:
        far_bucket = far_bucket + (magnitude >= boundary).astype(jnp.int32)
    bucket_near = jnp.where(magnitude < 8, magnitude, far_bucket)
    return bucket_near + 16 * (distance > 0).astype(jnp.int32)

def rms_norm(values, gain_row):
    return values * lax.rsqrt(lax.optimization_barrier(jnp.mean(values * values, axis=-1, keepdims=True)) + epsilon) * gain_row

def attend_sequence(normed, qkv_weight, output_weight, bias_full):
    seq_len = normed.shape[0]
    projected = low_back(low(jnp.dot(normed, qkv_weight, precision=top_expert_index)))
    split_rows = projected.reshape(seq_len, 3, HEADS, HEAD_DIM)
    query_key = jnp.einsum('qhd,khd->hqk', split_rows[:, 0], split_rows[:, 1], precision=top_expert_index) * score_scale
    scores = low_back(query_key) + bias_full
    raised = jnp.exp(scores - lax.optimization_barrier(jnp.max(scores, axis=-1, keepdims=True)))
    weights = low(raised / lax.optimization_barrier(jnp.sum(raised, axis=-1, keepdims=True)))
    mixed = jnp.einsum('hqk,khd->qhd', weights, split_rows[:, 2], precision=top_expert_index).reshape(seq_len, HEADS * HEAD_DIM)
    mixed = low_back(low(mixed))
    return low_back(jnp.dot(mixed, output_weight, precision=top_expert_index))

def expert_apply(pieces):
    slot_rows, weight_in, weight_out = pieces
    pre_act = low_back(jnp.einsum('rd,fd->rf', slot_rows, weight_in, precision=top_expert_index))
    activation = low(smooth_unit(pre_act))
    return low_back(low(jnp.einsum('rf,fd->rd', activation, weight_out, precision=top_expert_index)))

def dispatch_table(routes):
    blocks = routes.reshape(-1, TOK_SEQ)
    chosen_int = (blocks[:, :, None] == jnp.arange(EXPERTS, dtype=jnp.int32)).astype(jnp.int32)
    before = jnp.cumsum(chosen_int, axis=1) - chosen_int
    slot_index = lax.optimization_barrier(jnp.sum(before * chosen_int, axis=-1))
    target = blocks * CAP + slot_index
    return (target[:, :, None] == jnp.arange(EXPERTS * CAP, dtype=jnp.int32)).astype(jnp.float32)

def forward(tokens, attn_gain, qkv_weight, output_weight, bias_table, ffn_gain, router_projection_weight, expert_in, expert_out, dispatch, chosen):
    positions = jnp.arange(LENGTH, dtype=jnp.int32)
    bucket_grid = bucket_of(positions[None, :] - positions[:, None])
    bias_full = jnp.transpose(bias_table.reshape(BUCKETS, HEADS)[bucket_grid], (2, 0, 1))
    normed_one = low(rms_norm(tokens, attn_gain))

    def per_sequence(running, normed_seq):
        return (running, attend_sequence(normed_seq, qkv_weight, output_weight, bias_full))
    unused, branch = lax.scan(jax.checkpoint(per_sequence), jnp.zeros((), jnp.float32), normed_one)
    hidden = tokens + branch
    second_normed_input = low(rms_norm(hidden, ffn_gain))
    router_logits = jnp.einsum('ypk,km->ypm', second_normed_input, router_projection_weight, precision=top_expert_index)
    raised = jnp.exp(router_logits - lax.optimization_barrier(jnp.max(router_logits, axis=-1, keepdims=True)))
    chances = raised / lax.optimization_barrier(jnp.sum(raised, axis=-1, keepdims=True))
    gating = lax.optimization_barrier(jnp.sum(chances * chosen, axis=-1))
    slot_rows = jnp.einsum('ntc,ntd->ncd', dispatch, second_normed_input.reshape(-1, TOK_SEQ, D), precision=top_expert_index)
    grouped = jnp.transpose(slot_rows.reshape(-1, EXPERTS, CAP, D), (1, 0, 2, 3)).reshape(EXPERTS, -1, D)
    results = lax.map(jax.checkpoint(expert_apply), (grouped, jnp.transpose(expert_in, (1, 0, 2)), jnp.transpose(expert_out, (1, 0, 2))))
    returned = jnp.transpose(results.reshape(EXPERTS, -1, CAP, D), (1, 0, 2, 3)).reshape(-1, EXPERTS * CAP, D)
    combined = jnp.einsum('ntc,ncd->ntd', dispatch, returned, precision=top_expert_index).reshape(tokens.shape)
    return hidden + gating[..., None] * combined

def reference(tokens, cotangent, expert_ids, attn_gain, qkv_weight, output_weight, bias_table, ffn_gain, router_projection_weight, expert_in, expert_out):
    routes = expert_ids[..., 0]
    chosen = (routes[..., None] == jnp.arange(EXPERTS, dtype=jnp.int32)).astype(jnp.float32)
    dispatch = dispatch_table(routes)

    def run_layer(*floats):
        return forward(*floats, dispatch, chosen)
    floats = tuple((array.astype(jnp.float32) for array in (tokens, attn_gain, qkv_weight, output_weight, bias_table, ffn_gain, router_projection_weight, expert_in, expert_out)))
    result, pullback = jax.vjp(run_layer, *floats)
    grads = pullback(cotangent.astype(jnp.float32))
    return (result.astype(jnp.bfloat16), grads[0].astype(jnp.bfloat16), grads[1], grads[2], grads[3], grads[4], grads[5], grads[6], grads[7], grads[8])
```

```python
import functools

import jax
import jax.numpy as jnp
from jax import lax
from jax.experimental import pallas as pl
from jax.experimental.pallas import tpu as pltpu
from jax.sharding import PartitionSpec as P

HEADS = 12
HEAD_DIM = 64
BUCKETS = 32
EXPERTS = 4
EPS = 1e-06
THRESHOLDS = (12, 16, 23, 32, 46, 64, 91)
SCORE_SCALE = 0.125
TILE = 128
BF = jnp.bfloat16
F32 = jnp.float32
VMEM_LIMIT = 48 * 1024 * 1024
GELU_A = 0.7978845608028654
GELU_B = 0.044715

VM = pl.BlockSpec(memory_space=pltpu.VMEM)
SM = pl.BlockSpec(memory_space=pltpu.SMEM)


def nn(a, b):
    return lax.dot_general(a, b, (((1,), (0,)), ((), ())), preferred_element_type=F32)


def nt(a, b):
    return lax.dot_general(a, b, (((1,), (1,)), ((), ())), preferred_element_type=F32)


def tn(a, b):
    return lax.dot_general(a, b, (((0,), (0,)), ((), ())), preferred_element_type=F32)


def bucket_of(distance):
    magnitude = jnp.abs(distance)
    far = jnp.full(distance.shape, 8, jnp.int32)
    for boundary in THRESHOLDS:
        far = far + (magnitude >= boundary).astype(jnp.int32)
    near = jnp.where(magnitude < 8, magnitude, far)
    return near + 16 * (distance > 0).astype(jnp.int32)


def band_buckets():
    row = lax.broadcasted_iota(jnp.int32, (TILE, 3 * TILE), 0)
    col = lax.broadcasted_iota(jnp.int32, (TILE, 3 * TILE), 1)
    return bucket_of(col - TILE - row)


def call(body, out_shape, in_specs, scratch=(), name=None, cost=None):
    return pl.pallas_call(
        body,
        out_shape=out_shape,
        in_specs=in_specs,
        out_specs=jax.tree.map(lambda _: VM, out_shape),
        scratch_shapes=list(scratch),
        compiler_params=pltpu.CompilerParams(vmem_limit_bytes=VMEM_LIMIT),
        name=name,
        cost_estimate=cost,
    )


def sds(shape, dtype):
    return jax.ShapeDtypeStruct(shape, dtype)


def band_kernel(heads, tab_ref, out_ref):
    buckets = band_buckets()
    for h in range(heads):
        out_ref[h] = jnp.zeros((TILE, 3 * TILE), F32)

    def step(b, carry):
        hit = buckets == b
        for h in range(heads):
            out_ref[h] = jnp.where(hit, tab_ref[b, h], out_ref[h])
        return carry

    lax.fori_loop(0, BUCKETS, step, 0)


def tile_scores(q, k, band_ref, tab_ref, h, qi, tiles):
    raw = nt(q, k)
    lo, hi = TILE * max(0, qi - 1), TILE * min(tiles, qi + 2)
    off = TILE - (TILE * qi - lo)
    parts = []
    if lo > 0:
        parts.append(raw[:, :lo] + tab_ref[BUCKETS // 2 - 1, h])
    parts.append(raw[:, lo:hi] + band_ref[h, :, off : off + hi - lo])
    if hi < TILE * tiles:
        parts.append(raw[:, hi:] + tab_ref[BUCKETS - 1, h])
    return jnp.concatenate(parts, axis=1) if len(parts) > 1 else parts[0]


def attend_kernel(n, heads, *refs):
    me_ref, tab_ref = refs[:2]
    xs = refs[2 : 2 + n]
    gain_ref, w_ref, band_ref = refs[2 + n : 5 + n]
    n1_ref, qkv_ref, lse_ref = refs[5 + n : 8 + n]
    outs = refs[8 + n : 8 + 2 * n]
    a_scr = refs[8 + 2 * n]
    me = me_ref[0]
    rows = xs[0].shape[0]
    tiles = n * rows // TILE
    width = 3 * heads * HEAD_DIM
    for k in range(n):
        start = pl.multiple_of(lax.rem(me + n - k, n) * rows, rows)
        x = xs[k][...].astype(F32)
        scale = lax.rsqrt(jnp.mean(x * x, axis=-1, keepdims=True) + EPS)
        normed = (x * scale * gain_ref[...]).astype(BF)
        n1_ref[pl.ds(start, rows), :] = normed
        qkv = nn(normed, w_ref[...])[:, :width].astype(BF)
        for c in range(3 * heads):
            qkv_ref[c, pl.ds(start, rows), :] = qkv[:, HEAD_DIM * c : HEAD_DIM * (c + 1)]

    def head(h, carry):
        keys = qkv_ref[heads + h]
        values = qkv_ref[2 * heads + h]
        for qi in range(tiles):
            at = slice(TILE * qi, TILE * (qi + 1))
            q = qkv_ref[h, at, :] * jnp.asarray(SCORE_SCALE, BF)
            s = tile_scores(q, keys, band_ref, tab_ref, h, qi, tiles)
            top = jnp.max(s, axis=-1, keepdims=True)
            raised = jnp.exp(s - top)
            total = jnp.sum(raised, axis=-1, keepdims=True)
            weights = (raised * (1.0 / total)).astype(BF)
            a_scr[h, at, :] = nn(weights, values)
            lse_ref[h, at, :] = top + jnp.log(total)
        return carry

    lax.fori_loop(0, heads, head, 0)
    for k in range(n):
        start = pl.multiple_of(lax.rem(me + k, n) * rows, rows)
        outs[k][...] = jnp.concatenate(
            [a_scr[h, pl.ds(start, rows), :] for h in range(heads)], axis=1
        ).astype(BF)


def before_kernel(n, cap, share, *refs):
    me_ref, x_ref, g_ref = refs[:3]
    a_refs = refs[3 : 3 + n]
    wo_ref, gain_ref, router_ref, idc_ref, idr_ref = refs[3 + n : 8 + n]
    y1_ref, probs_ref, target_ref = refs[8 + n : 11 + n]
    outs = refs[11 + n : 11 + 2 * n]
    me = me_ref[0]
    rows = x_ref.shape[0]
    hd = a_refs[0].shape[1]
    y1 = x_ref[...].astype(F32)
    for k in range(n):
        start = pl.multiple_of(lax.rem(me + n - k, n) * hd, hd)
        y1 = y1 + nn(a_refs[k][...], wo_ref[pl.ds(start, hd), :])
    y1_ref[...] = y1
    scale = lax.rsqrt(jnp.mean(y1 * y1, axis=-1, keepdims=True) + EPS)
    n2 = (y1 * scale * gain_ref[...]).astype(BF)
    lane = lax.broadcasted_iota(jnp.int32, (rows, TILE), 1)
    logits = jnp.where(lane < EXPERTS, nn(n2, router_ref[...]), -1e30)
    raised = jnp.exp(logits - jnp.max(logits, axis=-1, keepdims=True))
    raised = jnp.where(lane < EXPERTS, raised, 0.0)
    probs = raised / jnp.sum(raised, axis=-1, keepdims=True)
    probs_ref[...] = probs
    hot = lane == idc_ref[...]
    gating = jnp.sum(jnp.where(hot, probs, 0.0), axis=-1, keepdims=True)
    hot = hot.astype(F32)
    r0 = lax.broadcasted_iota(jnp.int32, (rows, rows), 0)
    r1 = lax.broadcasted_iota(jnp.int32, (rows, rows), 1)
    earlier = nn((r1 < r0).astype(BF), hot.astype(BF))
    slot = jnp.sum(earlier * hot, axis=-1, keepdims=True)
    target_ref[...] = idc_ref[...].astype(F32) * cap + slot
    hot_t = (lax.broadcasted_iota(jnp.int32, (16, rows), 0) == idr_ref[...]).astype(F32)
    earlier_t = nn(hot_t.astype(BF), (r0 < r1).astype(BF))
    slot_t = jnp.sum(earlier_t * hot_t, axis=0, keepdims=True)
    target_t = idr_ref[...].astype(F32) * cap + slot_t
    slot_grad = (gating * g_ref[...].astype(F32)).astype(BF)
    place = lax.broadcasted_iota(jnp.int32, (cap, rows), 0)
    for k in range(n):
        first = lax.div(lax.rem(me + k, n), share) * cap
        pick = (target_t == (first + place).astype(F32)).astype(BF)
        outs[k][0] = nn(pick, n2).astype(BF)
        outs[k][1] = nn(pick, slot_grad).astype(BF)


def gelu_parts(z):
    square = z * z
    t = jnp.tanh(GELU_A * (z + GELU_B * square * z))
    half = 0.5 * (1.0 + t)
    slope = half + 0.5 * z * (1.0 - t * t) * (GELU_A * (1.0 + 3.0 * GELU_B * square))
    return z * half, slope


def expert_kernel(f, n, block, rows_ref, *refs):
    w_refs = refs[:f]
    outs = refs[f : f + n]
    eo, dx = refs[f + n :]
    cap = outs[0].shape[1]
    eo[...] = jnp.zeros_like(eo)
    dx[...] = jnp.zeros_like(dx)
    for w in w_refs:

        def step(j, carry, w=w):
            at = pl.ds(pl.multiple_of(j * block, block), block)
            w_in, w_out = w[0, at, :], w[1, at, :]
            act, slope = gelu_parts(nt(rows_ref[0], w_in))
            back = (nt(rows_ref[1], w_out) * slope).astype(BF)
            eo[...] += nn(act.astype(BF), w_out)
            dx[...] += nn(back, w_in)
            return carry

        lax.fori_loop(0, w.shape[1] // block, step, 0)
    for k in range(n):
        outs[k][0] = eo[cap * k : cap * (k + 1), :].astype(BF)
        outs[k][1] = dx[cap * k : cap * (k + 1), :].astype(BF)


def expert_grad_kernel(f, block, *refs):
    row_refs = refs[:f]
    w_ref, out_ref, xin, deo = refs[f:]
    count = row_refs[0].shape[1]
    for i in range(f):
        xin[count * i : count * (i + 1), :] = row_refs[i][0]
        deo[count * i : count * (i + 1), :] = row_refs[i][1]

    def step(j, carry):
        at = pl.ds(pl.multiple_of(j * block, block), block)
        act, slope = gelu_parts(nt(w_ref[0, at, :], xin[...]))
        back = (nt(w_ref[1, at, :], deo[...]) * slope).astype(BF)
        out_ref[0, at, :] = nn(back, xin[...]).astype(BF)
        out_ref[1, at, :] = nn(act.astype(BF), deo[...]).astype(BF)
        return carry

    lax.fori_loop(0, w_ref.shape[1] // block, step, 0)


def after_kernel(n, cap, share, *refs):
    me_ref, g_ref, y1_ref, probs_ref, target_ref, idc_ref = refs[:6]
    back_refs = refs[6 : 6 + n]
    a_refs = refs[6 + n : 6 + 2 * n]
    wo_ref, gain_ref, router_ref = refs[6 + 2 * n : 9 + 2 * n]
    out_ref, dy1_ref, gwo_ref, small_ref = refs[9 + 2 * n : 13 + 2 * n]
    outs = refs[13 + 2 * n :]
    me = me_ref[0]
    rows = g_ref.shape[0]
    hd = a_refs[0].shape[1]
    y1 = y1_ref[...]
    g = g_ref[...].astype(F32)
    scale = lax.rsqrt(jnp.mean(y1 * y1, axis=-1, keepdims=True) + EPS)
    unit = y1 * scale
    n2 = (unit * gain_ref[...]).astype(BF)
    lane = lax.broadcasted_iota(jnp.int32, (rows, TILE), 1)
    hot = (lane == idc_ref[...]).astype(F32)
    probs = probs_ref[...]
    gating = jnp.sum(probs * hot, axis=-1, keepdims=True)
    place = lax.broadcasted_iota(jnp.int32, (rows, cap), 1)
    combined = jnp.zeros((rows, y1.shape[1]), F32)
    dn2 = jnp.zeros((rows, y1.shape[1]), F32)
    for k in range(n):
        first = lax.div(lax.rem(me + k, n), share) * cap
        pick = (target_ref[...] == (first + place).astype(F32)).astype(BF)
        combined = combined + nn(pick, back_refs[k][0])
        dn2 = dn2 + nn(pick, back_refs[k][1])
    out_ref[...] = (y1 + gating * combined).astype(BF)
    gate_grad = jnp.sum(g * combined, axis=-1, keepdims=True)
    dlogits = (gating * gate_grad) * (hot - probs)
    for e in range(EXPERTS):
        dn2 = dn2 + dlogits[:, e : e + 1] * router_ref[e : e + 1, :]
    high = dlogits.astype(BF)
    low = (dlogits - high.astype(F32)).astype(BF)
    router_grad = tn(high, n2) + tn(low, n2)
    small_ref[0:8, :] = router_grad[0:8, :]
    small_ref[8:16, :] = jnp.broadcast_to(
        jnp.sum(dn2 * unit, axis=0, keepdims=True), (8, y1.shape[1])
    )
    scaled = dn2 * gain_ref[...]
    inner = jnp.mean(scaled * unit, axis=-1, keepdims=True)
    dy1 = g + scale * (scaled - unit * inner)
    dy1_ref[...] = dy1
    db = dy1.astype(BF)
    for k in range(n):
        start = pl.multiple_of(lax.rem(me + k, n) * hd, hd)
        outs[k][...] = nt(db, wo_ref[pl.ds(start, hd), :]).astype(BF)
    for k in range(n):
        start = pl.multiple_of(lax.rem(me + n - k, n) * hd, hd)
        gwo_ref[pl.ds(start, hd), :] = tn(a_refs[k][...], db)


def attend_back_kernel(n, heads, *refs):
    me_ref, tab_ref = refs[:2]
    das = refs[2 : 2 + n]
    qkv_ref, lse_ref, band_ref = refs[2 + n : 5 + n]
    full_ref, bias_ref = refs[5 + n : 7 + n]
    outs = refs[7 + n : 7 + 2 * n]
    da_scr, grads, key_t, value_t, acc, left, right = refs[7 + 2 * n :]
    me = me_ref[0]
    rows = das[0].shape[0]
    tiles = n * rows // TILE
    buckets = band_buckets()
    for k in range(n):
        start = pl.multiple_of(lax.rem(me + n - k, n) * rows, rows)
        for h in range(heads):
            da_scr[h, pl.ds(start, rows), :] = das[k][:, HEAD_DIM * h : HEAD_DIM * (h + 1)]

    def head(h, carry):
        keys = qkv_ref[heads + h]
        values = qkv_ref[2 * heads + h]
        key_t[...] = jnp.zeros_like(key_t)
        value_t[...] = jnp.zeros_like(value_t)
        acc[...] = jnp.zeros_like(acc)
        left[...] = jnp.zeros_like(left)
        right[...] = jnp.zeros_like(right)
        for qi in range(tiles):
            at = slice(TILE * qi, TILE * (qi + 1))
            q = qkv_ref[h, at, :] * jnp.asarray(SCORE_SCALE, BF)
            da = da_scr[h, at, :]
            s = tile_scores(q, keys, band_ref, tab_ref, h, qi, tiles)
            p = jnp.exp(s - lse_ref[h, at, :])
            dp = nt(da, values)
            dot = jnp.sum(p * dp, axis=-1, keepdims=True)
            ds = p * (dp - dot)
            low = ds.astype(BF)
            grads[h, at, :] = nn(low, keys) * SCORE_SCALE
            key_t[...] += tn(q, low)
            value_t[...] += tn(da, p.astype(BF))
            lo, hi = max(0, qi - 1), min(tiles, qi + 2)
            off = TILE - TILE * (qi - lo)
            acc[:, off : off + TILE * (hi - lo)] += ds[:, TILE * lo : TILE * hi]
            if lo > 0:
                left[...] += sum(ds[:, TILE * b : TILE * (b + 1)] for b in range(lo))
            if hi < tiles:
                right[...] += sum(ds[:, TILE * b : TILE * (b + 1)] for b in range(hi, tiles))
        grads[heads + h] = key_t[...].T
        grads[2 * heads + h] = value_t[...].T
        for b in range(BUCKETS):
            line = jnp.sum(jnp.where(buckets == b, acc[...], 0.0), axis=0, keepdims=True)
            line = line[:, :TILE] + line[:, TILE : 2 * TILE] + line[:, 2 * TILE :]
            if b == BUCKETS // 2 - 1:
                line = line + jnp.sum(left[...], axis=0, keepdims=True)
            if b == BUCKETS - 1:
                line = line + jnp.sum(right[...], axis=0, keepdims=True)
            bias_ref[h, b : b + 1, :] = line
        return carry

    lax.fori_loop(0, heads, head, 0)
    for k in range(n):
        start = pl.multiple_of(lax.rem(me + k, n) * rows, rows)
        piece = jnp.concatenate(
            [grads[c, pl.ds(start, rows), :] for c in range(3 * heads)], axis=1
        ).astype(BF)
        outs[k][...] = piece
        full_ref[pl.ds(start, rows), :] = piece


def input_kernel(n, *refs):
    me_ref, x_ref, dy1_ref = refs[:3]
    ds = refs[3 : 3 + n]
    w_ref, gain_ref, out_ref = refs[3 + n :]
    me = me_ref[0]
    x = x_ref[...].astype(F32)
    scale = lax.rsqrt(jnp.mean(x * x, axis=-1, keepdims=True) + EPS)
    unit = x * scale
    dn1 = jnp.zeros(x.shape, F32)
    for k in range(n):
        dn1 = dn1 + nt(ds[k][...], w_ref[lax.rem(me + n - k, n)])
    scaled = dn1 * gain_ref[...]
    inner = jnp.mean(scaled * unit, axis=-1, keepdims=True)
    out_ref[...] = (dy1_ref[...] + scale * (scaled - unit * inner)).astype(BF)


def shift(value, n, k, axis="seq"):
    if k % n == 0:
        return value
    return lax.ppermute(value, axis, [(i, (i + k) % n) for i in range(n)])


def swap(value, n, bit, axis):
    return lax.ppermute(value, axis, [(i, i ^ bit) for i in range(n)])


def ahead_to_order(pieces, me):
    n = len(pieces)
    both = jnp.stack(pieces + pieces)
    return lax.dynamic_slice_in_dim(both, lax.rem(n - me, n), n, 0)


def behind_to_order(pieces, me):
    n = len(pieces)
    both = jnp.stack(pieces[::-1] + pieces[::-1])
    return lax.dynamic_slice_in_dim(both, n - 1 - me, n, 0)


def bits_of(n):
    return [1 << b for b in range(n.bit_length() - 1)]


def gather_swap(value, n, axis):
    pieces = [value]
    order = [0]
    for bit in reversed(bits_of(n)):
        pieces = pieces + [swap(p, n, bit, axis) for p in pieces]
        order = order + [m | bit for m in order]
    return [pieces[order.index(m)] for m in range(n)]


def swap_to_order(pieces, own):
    stacked = jnp.stack(pieces)
    return jnp.stack(
        [
            lax.dynamic_index_in_dim(stacked, jnp.bitwise_xor(i, own), 0, keepdims=False)
            for i in range(len(pieces))
        ]
    )


def scatter_swap(value, n, own, axis):
    for bit in bits_of(n):
        side = lax.rem(lax.div(own, bit), 2)
        paired = value.reshape((value.shape[0] // 2, 2) + value.shape[1:])
        keep = lax.dynamic_index_in_dim(paired, side, 1, keepdims=False)
        send = lax.dynamic_index_in_dim(paired, 1 - side, 1, keepdims=False)
        value = keep + swap(send.astype(BF), n, bit, axis).astype(F32)
    return value[0]


def scatter_seq(value, n, me):
    total = lax.dynamic_index_in_dim(value, me, 0, keepdims=False)
    for k in range(1, n):
        block = lax.dynamic_index_in_dim(value, lax.rem(me + k, n), 0, keepdims=False)
        total = total + shift(block.astype(BF), n, k).astype(F32)
    return total


def over_replica(value, n):
    low = value.astype(BF)
    if n == 1:
        return value
    if n == 2:
        return low.astype(F32) + swap(low, 2, 1, "replica").astype(F32)
    return lax.psum(low, "replica").astype(F32)


def per_device(
    tokens,
    cotangent,
    expert_ids,
    attn_gain,
    qkv_weight,
    output_weight,
    bias_table,
    ffn_gain,
    router_weight,
    expert_in,
    expert_out,
):
    _, rows, width = tokens.shape
    n, f, copies = lax.axis_size("seq"), lax.axis_size("fsdp"), lax.axis_size("replica")
    me, mine = lax.axis_index("seq"), lax.axis_index("fsdp")
    length = n * rows
    heads = -(-HEADS // n)
    hd = heads * HEAD_DIM
    total_hd = n * hd
    share = n // EXPERTS
    slots = rows * 5 // (4 * EXPERTS)
    cap = -(-slots // 16) * 16
    shard = qkv_weight.shape[0]
    unit_count = expert_in.shape[0]
    part = unit_count // share
    quarter = n * part
    block = 256 if quarter % 256 == 0 else quarter
    packed_width = -(-(3 * hd + 7) // TILE) * TILE
    me_arr = me.reshape(1)
    x = tokens[0]
    g = cotangent[0]
    ids = expert_ids[0]
    others = range(1, n)

    xs = [x] + [shift(x, n, k) for k in others]

    by_head = jnp.pad(qkv_weight.reshape(shard, 3, width), ((0, 0), (0, 0), (0, total_hd - width)))
    by_head = by_head.reshape(shard, 3, n, hd).transpose(2, 0, 1, 3).reshape(n, shard, 3 * hd)
    table_part = bias_table.shape[0]
    small = jnp.concatenate(
        [
            attn_gain[:, None],
            ffn_gain[:, None],
            router_weight,
            jnp.pad(bias_table, (0, shard - table_part))[:, None],
            jnp.zeros((shard, packed_width - 3 * hd - 7), BF),
        ],
        axis=1,
    )
    packed = jnp.concatenate(
        [by_head, jnp.broadcast_to(small[None], (n,) + small.shape)], axis=2
    )
    chunks = [
        shift(lax.dynamic_index_in_dim(packed, lax.rem(me + k, n), 0, keepdims=False), n, k)
        for k in range(n)
    ]
    chunk_rows = behind_to_order(chunks, me).reshape(n * shard, packed_width)
    own_w = swap_to_order(gather_swap(chunk_rows, f, "fsdp"), mine).reshape(width, packed_width)
    tail = own_w[:, 3 * hd : 3 * hd + 7]
    gain_one = tail[:, 0].astype(F32).reshape(1, width)
    gain_two = tail[:, 1].astype(F32).reshape(1, width)
    router = tail[:, 2 : 2 + EXPERTS]
    router_lanes = jnp.pad(router, ((0, 0), (0, TILE - EXPERTS)))
    router_rows = jnp.pad(router.astype(F32).T, ((0, 8 - EXPERTS), (0, 0)))
    table = tail[:, 6].reshape(f * n, shard)[:, :table_part].reshape(BUCKETS, HEADS).astype(F32)
    table = lax.dynamic_slice_in_dim(
        jnp.pad(table, ((0, 0), (0, n * heads - HEADS))), me * heads, heads, 1
    )
    band = call(
        functools.partial(band_kernel, heads),
        sds((heads, TILE, 3 * TILE), F32),
        [SM],
        name="bias_band",
    )(table)

    def expert_chunk(weight, k):
        dst = lax.rem(me + k, n)
        cut = lax.dynamic_slice(
            weight.reshape(share, part, EXPERTS, width),
            (lax.rem(dst, share), 0, lax.div(dst, share), 0),
            (1, part, 1, width),
        )
        return cut.reshape(part, width)

    pieces = [
        shift(jnp.stack([expert_chunk(expert_in, k), expert_chunk(expert_out, k)]), n, k)
        for k in range(n)
    ]
    own_expert = jnp.concatenate(pieces, axis=1)
    expert_parts = gather_swap(own_expert, f, "fsdp")

    wo = lax.all_gather(output_weight, ("fsdp", "seq"), axis=0, tiled=True)
    wo = jnp.pad(wo, ((0, total_hd - width), (0, 0)))
    wq = lax.all_gather(qkv_weight, ("fsdp", "seq"), axis=0, tiled=True)
    wq = jnp.pad(wq.reshape(width, 3, width), ((0, 0), (0, 0), (0, total_hd - width)))
    wq = wq.reshape(width, 3, n, hd).transpose(2, 0, 1, 3).reshape(n, width, 3 * hd)

    attended = call(
        functools.partial(attend_kernel, n, heads),
        [
            sds((length, width), BF),
            sds((3 * heads, length, HEAD_DIM), BF),
            sds((heads, length, 1), F32),
        ]
        + [sds((rows, hd), BF)] * n,
        [SM, SM] + [VM] * (n + 3),
        [pltpu.VMEM((heads, length, HEAD_DIM), F32)],
        name="attend",
    )(me_arr, table, *xs, gain_one, own_w, band)
    n1, qkv, lse = attended[:3]
    mixed = [shift(attended[3 + k], n, k) for k in range(n)]

    before = call(
        functools.partial(before_kernel, n, cap, share),
        [sds((rows, width), F32), sds((rows, TILE), F32), sds((rows, 1), F32)]
        + [sds((2, cap, width), BF)] * n,
        [SM] + [VM] * (n + 7),
        name="before_experts",
    )(me_arr, x, g, *mixed, wo, gain_two, router_lanes, ids, ids.reshape(1, rows))
    y1, probs, target = before[:3]
    arrived = [shift(before[3 + k], n, k) for k in range(n)]
    expert_rows = jnp.concatenate(arrived, axis=1)

    results = call(
        functools.partial(expert_kernel, f, n, block),
        [sds((2, cap, width), BF)] * n,
        [VM] * (f + 1),
        [pltpu.VMEM((n * cap, width), F32)] * 2,
        name="experts",
    )(expert_rows, *expert_parts)
    returned = [shift(results[k], n, n - k) for k in range(n)]

    all_rows = gather_swap(expert_rows, f, "fsdp")
    expert_grad = call(
        functools.partial(expert_grad_kernel, f, block),
        sds((2, quarter, width), BF),
        [VM] * (f + 1),
        [pltpu.VMEM((f * n * cap, width), BF)] * 2,
        name="expert_grads",
    )(*all_rows, own_expert)
    home = [
        shift(expert_grad[:, part * k : part * (k + 1), :], n, n - k) for k in range(n)
    ]
    home = [over_replica(piece, copies) for piece in home]
    home = ahead_to_order(home, me).reshape(EXPERTS, share, 2, part, width)
    home = home.transpose(2, 1, 3, 0, 4).reshape(2, unit_count, EXPERTS, width)

    after = call(
        functools.partial(after_kernel, n, cap, share),
        [
            sds((rows, width), BF),
            sds((rows, width), F32),
            sds((total_hd, width), F32),
            sds((16, width), F32),
        ]
        + [sds((rows, hd), BF)] * n,
        [SM] + [VM] * (2 * n + 8),
        name="after_experts",
    )(me_arr, g, y1, probs, target, ids, *returned, *mixed, wo, gain_two, router_rows)
    layer_out, dy1, wo_grad, small_grad = after[:4]
    das = [shift(after[4 + k], n, k) for k in range(n)]

    back = call(
        functools.partial(attend_back_kernel, n, heads),
        [sds((length, 3 * hd), BF), sds((heads, BUCKETS, TILE), F32)]
        + [sds((rows, 3 * hd), BF)] * n,
        [SM, SM] + [VM] * (n + 3),
        [
            pltpu.VMEM((heads, length, HEAD_DIM), BF),
            pltpu.VMEM((3 * heads, length, HEAD_DIM), F32),
            pltpu.VMEM((HEAD_DIM, length), F32),
            pltpu.VMEM((HEAD_DIM, length), F32),
            pltpu.VMEM((TILE, 3 * TILE), F32),
            pltpu.VMEM((TILE, TILE), F32),
            pltpu.VMEM((TILE, TILE), F32),
        ],
        name="attend_back",
    )(me_arr, table, *das, qkv, lse, band)
    dqkv, bias_lines = back[:2]
    own_dqkv = [shift(back[2 + k], n, k) for k in range(n)]
    input_grad = call(
        functools.partial(input_kernel, n),
        sds((rows, width), BF),
        [SM] + [VM] * (n + 4),
        name="input_grad",
    )(me_arr, x, dy1, *own_dqkv, wq, gain_one)

    qkv_grad = jnp.einsum("td,te->de", n1, dqkv, preferred_element_type=F32)
    qkv_grad = scatter_swap(qkv_grad.reshape(f, n, shard, 3 * hd), f, mine, "fsdp").astype(BF)
    qkv_grad = over_replica(qkv_grad, copies).astype(BF)
    qkv_grad = [
        shift(lax.dynamic_index_in_dim(qkv_grad, lax.rem(me + k, n), 0, keepdims=False), n, k)
        for k in range(n)
    ]
    qkv_grad = behind_to_order(qkv_grad, me).reshape(n, shard, 3, hd).transpose(1, 2, 0, 3)
    qkv_grad = qkv_grad.reshape(shard, 3, total_hd)[:, :, :width].reshape(shard, 3 * width)
    qkv_grad = qkv_grad.astype(F32)
    gain_one_grad = jnp.sum(qkv_grad * qkv_weight.astype(F32), axis=1) / attn_gain.astype(F32)

    wo_grad = wo_grad[:width].reshape(f, n, shard, width)
    wo_grad = scatter_swap(wo_grad, f, mine, "fsdp")
    wo_grad = over_replica(scatter_seq(wo_grad, n, me), copies)

    bias_rows = jnp.sum(bias_lines, axis=-1).T
    bias_rows = lax.dynamic_update_slice_in_dim(
        jnp.zeros((BUCKETS, n * heads), F32), bias_rows, me * heads, 1
    )[:, :HEADS].reshape(-1)
    sums = jnp.concatenate(
        [
            small_grad[: EXPERTS + 0],
            small_grad[8:9],
            jnp.pad(bias_rows, (0, width - BUCKETS * HEADS))[None],
        ],
        axis=0,
    )
    for axis, size in (("fsdp", f), ("replica", copies), ("seq", n)):
        for bit in bits_of(size):
            sums = sums + swap(sums, size, bit, axis)
    owner = mine * n + me
    router_grad = lax.dynamic_slice_in_dim(sums[:EXPERTS].T, owner * shard, shard, 0)
    gain_two_grad = lax.dynamic_slice_in_dim(sums[EXPERTS], owner * shard, shard, 0)
    bias_grad = lax.dynamic_slice_in_dim(sums[EXPERTS + 1], owner * table_part, table_part, 0)

    return (
        layer_out[None],
        input_grad[None],
        gain_one_grad,
        qkv_grad,
        wo_grad,
        bias_grad,
        gain_two_grad,
        router_grad,
        home[0],
        home[1],
    )


def solution(mesh):
    rows = P(("replica", "fsdp"), "seq", None)
    one, two, three = P(("fsdp", "seq")), P(("fsdp", "seq"), None), P(("fsdp", "seq"), None, None)
    return jax.shard_map(
        per_device,
        mesh=mesh,
        in_specs=(rows, rows, rows, one, two, two, one, one, two, three, three),
        out_specs=(rows, rows, one, two, two, one, one, two, three, three),
        check_vma=False,
    )
```
